256 devices in a mesh: segment: 2 (over core), dom: 32 (over x, z), rep: 4 (over y).
Axes of the slice: x: 4, y: 4, z: 8, core: 2. Of those that a mesh axis runs over, the one named last changes fastest.
Arguments:
- features: bfloat16 [4, 2, 8192, 512], P('rep', None, 'dom'), may hold values from -6 to 6
- tile_vals: bfloat16 [4, 2, 192, 128, 128], P('rep', None, 'dom'), may hold values from -0.3125 to 0.3125
- tile_cols: int32 [4, 2, 192], P('rep', None, 'dom'), may hold values from 0 to 3, as said below
- send_lists: int32 [4, 2, 64, 1], P('rep', None, 'dom'), may hold values from 0 to 1
- section_layers: int32 [2], replicated, may hold values from 1 to 2, as said below
- weights: bfloat16 [4, 512, 512], P('segment'), may hold values from -0.25 to 0.25
- cotangent: bfloat16 [4, 2, 8192, 512], P('rep', None, 'dom'), may hold values from -0.1875 to 0.1875
Outputs:
- weight_grads: float32 [4, 512, 512], P('segment')
The draws below stay inside these ranges and needn't reach their ends.
Inputs may be any that keep to these rules, and one draw needn't show every extreme that they name: `tile_cols`: in each row block's group of 3 tiles the first names the row block itself, the second a received block, and every received block of a partition is named by some second tile; the rest name any block. `section_layers`: one section has exactly 2 layers.
All inputs are finite; a program needn't handle non-finite values.
Results may differ from the reference program's by a relative error of at most 0.02.
Values may be sent and summed in bfloat16 or wider, within the bound.
No kernel may reach another device: no remote copies, remote signals or barrier semaphores. Data moves between devices by JAX's collectives and lax.ppermute only.
A program may use at most 64 MiB of HBM per device.

```python
import jax
import jax.numpy as jnp
from jax import lax

D = 512
BLOCK = 128
TPR = 3
RB = 2
SLOTS = 2
MICRO = 2
HALO = 1
NT = 6
VERTS = 8192
N_SEGMENT = 2
N_DOM = 32
N_REP = 4


def draw_tile_cols(key, part):
    key = jax.random.fold_in(key, 11)
    key_offset, key_any = jax.random.split(key)
    groups = N_REP * MICRO * N_DOM
    offsets = jax.random.randint(key_offset, (groups, 1), 0, 2 * HALO)
    block_ids = jnp.arange(RB)[None, :]
    second = RB + (block_ids + offsets) % (2 * HALO)
    anywhere = jax.random.randint(key_any, (groups, RB, TPR), 0, RB + 2 * HALO)
    lane_ids = jnp.arange(TPR)[None, None, :]
    chosen = jnp.where(lane_ids == 0, block_ids[:, :, None], jnp.where(lane_ids == 1, second[:, :, None], anywhere))
    return chosen.reshape(N_REP, MICRO, N_DOM * RB * TPR).astype(jnp.int32)


def draw_section_layers(key, part):
    key = jax.random.fold_in(key, 23)
    key_pick, key_len = jax.random.split(key)
    longest = jax.random.randint(key_pick, (), 0, N_SEGMENT)
    lengths = jax.random.randint(key_len, (N_SEGMENT,), 1, SLOTS + 1)
    return jnp.where(jnp.arange(N_SEGMENT) == longest, SLOTS, lengths).astype(jnp.int32)


def place_ends(values, stream_key, least, high):
    extent = values.shape
    place = [jax.random.randint(jax.random.fold_in(stream_key, axis), (), 0, extent[axis]) for axis in range(len(extent))]
    values = values.at[tuple(place)].set(least)
    longest = extent.index(max(extent))
    place[longest] = (place[longest] + 1) % extent[longest]
    return values.at[tuple(place)].set(high)


def levels(rng, dims, pieces, smallest, largest):
    level = 1.0
    for axis_at, blocks in pieces:
        heights = jax.random.uniform(jax.random.fold_in(jax.random.fold_in(rng, 6), axis_at), (blocks,), jnp.float32, smallest / len(pieces), largest / len(pieces))
        level = level * jnp.repeat(jnp.exp(heights), dims[axis_at] // blocks).reshape((-1,) + (1,) * (len(dims) - 1 - axis_at))
    return level


def scatter_about(key, dims, width, limit, pieces=(), kind=jnp.bfloat16):
    drawn = jax.random.normal(key, dims, jnp.float32) * width
    if len(pieces) > 0:
        drawn = levels(key, dims, pieces, -0.22, 0.18) * drawn
    return jnp.clip(drawn, min=-limit, max=limit).astype(kind)


def setup_inputs(seed: int = 0) -> dict:
    key_list = jax.random.split(jax.random.key(seed), 8)
    features = scatter_about(key_list[0], (N_REP, MICRO, VERTS, D), 1.0, 6.0, ((0, 4), (2, 32)))
    tile_vals = scatter_about(key_list[1], (N_REP, MICRO, N_DOM * NT, BLOCK, BLOCK), (BLOCK * TPR) ** -0.5, 0.3125, ((0, 4), (2, 32)))
    tile_cols = draw_tile_cols(jax.random.fold_in(key_list[7], 71), 0)
    send_lists = place_ends(jax.random.randint(key_list[3], (N_REP, MICRO, N_DOM * 2, HALO), 0, RB), jax.random.fold_in(key_list[3], 1), 0, RB - 1).astype(jnp.int32)
    section_layers = draw_section_layers(jax.random.fold_in(key_list[7], 71), 0)
    weights = scatter_about(key_list[5], (N_SEGMENT * SLOTS, D, D), D ** -0.5, 0.25, ((0, 2),))
    cotangent = scatter_about(key_list[6], (N_REP, MICRO, VERTS, D), (3.0 * (N_REP * MICRO * VERTS) ** (-0.5)), 0.1875, ((0, 4), (2, 32)))
    return dict(features=features, tile_vals=tile_vals, tile_cols=tile_cols, send_lists=send_lists, section_layers=section_layers, weights=weights, cotangent=cotangent)


STRENGTH = 0.5
RESTART = 0.1

def gelu_tanh(value):
    return jax.nn.gelu(value, approximate=True)

def take_blocks(blocks, index):
    return jnp.take_along_axis(blocks, index.astype(jnp.int32)[:, :, None, None], axis=1)

def layer_forward(layer_in, initial, tile_now, col_now, send_now, weight, mixing, active):
    to_left = take_blocks(layer_in, send_now[:, 0])
    to_right = take_blocks(layer_in, send_now[:, 1])
    buffer = jnp.concatenate((layer_in, jnp.roll(to_right, 1, axis=0), jnp.roll(to_left, -1, axis=0)), axis=1)
    picked = take_blocks(buffer, col_now)
    products = jnp.einsum('ptij,ptjd->ptid', tile_now.astype(jnp.float32), picked.astype(jnp.float32), precision=lax.Precision.HIGHEST)
    merged = products.reshape(RB_PARTS(layer_in) + (TPR, BLOCK, D)).sum(axis=2)
    mixed_rows = ((1.0 - RESTART) * merged + RESTART * initial.astype(jnp.float32)).astype(jnp.bfloat16)
    projected = jnp.dot(mixed_rows.reshape(-1, D), weight, preferred_element_type=jnp.float32).reshape(mixed_rows.shape)
    hidden = (1.0 - mixing) * mixed_rows.astype(jnp.float32) + mixing * projected
    result = jnp.where(active, gelu_tanh(hidden).astype(jnp.bfloat16), layer_in)
    return (result, mixed_rows, hidden)

def RB_PARTS(layer_in):
    return (layer_in.shape[0], layer_in.shape[1])

def layer_backward(grad_out, mixed_rows, hidden, tile_now, col_now, send_now, weight, mixing, active):
    pullback = jax.vjp(gelu_tanh, hidden)[1]
    grad_hidden = jnp.where(active, pullback(grad_out)[0], jnp.zeros_like(grad_out))
    grad_round = grad_hidden.astype(jnp.bfloat16)
    weight_part = mixing * jnp.dot(mixed_rows.reshape(-1, D).T, grad_round.reshape(-1, D), preferred_element_type=jnp.float32)
    back_mix = jnp.dot(grad_round.reshape(-1, D), weight.T, preferred_element_type=jnp.float32).reshape(grad_out.shape)
    grad_mixed = (1.0 - mixing) * grad_hidden + mixing * back_mix
    grad_agg = ((1.0 - RESTART) * grad_mixed).astype(jnp.bfloat16)
    spread = jnp.repeat(grad_agg, TPR, axis=1)
    contrib = jnp.einsum('ptij,ptid->ptjd', tile_now.astype(jnp.float32), spread.astype(jnp.float32), precision=lax.Precision.HIGHEST)
    onehot = (col_now[:, :, None] == jnp.arange(RB + 2 * HALO, dtype=jnp.int32)[None, None, :]).astype(jnp.float32)
    grad_buffer = jnp.einsum('ptc,ptjd->pcjd', onehot, contrib, precision=lax.Precision.HIGHEST)
    from_left = grad_buffer[:, RB:RB + HALO]
    from_right = grad_buffer[:, RB + HALO:]
    for_right_list = jnp.roll(from_left, -1, axis=0)
    for_left_list = jnp.roll(from_right, 1, axis=0)
    left_hit = (send_now[:, 0, :, None] == jnp.arange(RB, dtype=jnp.int32)[None, None, :]).astype(jnp.float32)
    right_hit = (send_now[:, 1, :, None] == jnp.arange(RB, dtype=jnp.int32)[None, None, :]).astype(jnp.float32)
    own_grad = grad_buffer[:, :RB]
    own_grad = own_grad + jnp.einsum('phr,phjd->prjd', left_hit, for_left_list, precision=lax.Precision.HIGHEST)
    own_grad = own_grad + jnp.einsum('phr,phjd->prjd', right_hit, for_right_list, precision=lax.Precision.HIGHEST)
    grad_in = jnp.where(active, own_grad, grad_out)
    return (grad_in, weight_part)

def reference(features, tile_vals, tile_cols, send_lists, section_layers, weights, cotangent):
    item_count = N_REP * MICRO
    node_shape = (item_count, N_DOM, RB, BLOCK, D)
    feats = features.reshape(node_shape)
    cots = cotangent.reshape(node_shape)
    tiles_all = tile_vals.reshape(item_count, N_DOM, RB * TPR, BLOCK, BLOCK)
    cols_all = tile_cols.reshape(item_count, N_DOM, RB * TPR).astype(jnp.int32)
    sends_all = send_lists.reshape(item_count, N_DOM, 2, HALO).astype(jnp.int32)
    bases = jnp.cumsum(section_layers) - section_layers

    def one_item(grad_total, inputs):
        initial, tile_now, col_now, send_now, cot_now = inputs
        layer_in = initial
        saved = []
        for section in range(N_SEGMENT):
            for slot_num in range(SLOTS):
                active = slot_num < section_layers[section]
                layer_num = (bases[section] + slot_num + 1).astype(jnp.float32)
                mixing = jnp.log(STRENGTH / layer_num + 1.0)
                weight = weights[section * SLOTS + slot_num]
                layer_in, mixed_rows, hidden = layer_forward(layer_in, initial, tile_now, col_now, send_now, weight, mixing, active)
                saved.append((mixed_rows, hidden, weight, mixing, active))
        grad_now = cot_now.astype(jnp.float32)
        parts_list = [None] * len(saved)
        for index in reversed(range(len(saved))):
            mixed_rows, hidden, weight, mixing, active = saved[index]
            grad_now, weight_part = layer_backward(grad_now, mixed_rows, hidden, tile_now, col_now, send_now, weight, mixing, active)
            parts_list[index] = weight_part
        return (grad_total + jnp.stack(parts_list), None)
    start_total = jnp.zeros((N_SEGMENT * SLOTS, D, D), jnp.float32)
    grad_total, _ = lax.scan(one_item, start_total, (feats, tiles_all, cols_all, sends_all, cots))
    return grad_total
```

```python
import functools
import math

import jax
import jax.numpy as jnp
import numpy as np
from jax import lax
from jax.experimental import pallas as pl
from jax.experimental.pallas import tpu as pltpu
from jax.sharding import Mesh
from jax.sharding import PartitionSpec as P

BLOCK = 128
ROWS = 256
FEAT = 512
KEEP = 0.9
RESTART = 0.1
STRENGTH = 0.5
C0 = math.sqrt(2.0 / math.pi)
C1 = 0.044715
BF = jnp.bfloat16
F32 = jnp.float32
DOM = ("x", "z")
PLANE = ("x", "rep")


def beta(k):
    return float(np.log(np.float32(STRENGTH / k + 1.0)))


def spec(shape, dtype):
    return jax.ShapeDtypeStruct(shape, dtype)


def call(kernel, outs, scalars, arrays, name):
    smem = [pl.BlockSpec(memory_space=pltpu.SMEM)] * len(scalars)
    vmem = [pl.BlockSpec(memory_space=pltpu.VMEM)] * len(arrays)
    return pl.pallas_call(
        kernel,
        out_shape=outs,
        in_specs=smem + vmem,
        out_specs=jax.tree.map(lambda _: pl.BlockSpec(memory_space=pltpu.VMEM), outs),
        compiler_params=pltpu.CompilerParams(vmem_limit_bytes=40 * 1024 * 1024),
        name=name,
    )(*scalars, *arrays)


def mm(a, b):
    return jnp.dot(a, b, preferred_element_type=F32)


def mm_nt(a, b):
    return lax.dot_general(a, b, (((1,), (1,)), ((), ())), preferred_element_type=F32)


def mm_tn(a, b):
    return lax.dot_general(a, b, (((0,), (0,)), ((), ())), preferred_element_type=F32)


def first_kernel(scal, feats, to_left, to_right):
    micro = scal[0]
    to_left[...] = feats[micro, scal[7]]
    to_right[...] = feats[micro, scal[8]]


def prep_kernel(scal, tiles, feats, cot, rem, own, rem_t, own_t, base, feats_own, cot_own):
    micro = scal[0]
    zero = jnp.zeros((BLOCK, BLOCK), BF)
    for b in range(2):
        rows = pl.ds(b * BLOCK, BLOCK)
        first = tiles[micro, 3 * b].astype(F32)
        second = tiles[micro, 3 * b + 1].astype(F32)
        third = tiles[micro, 3 * b + 2].astype(F32)
        first_t, second_t, third_t = first.T, second.T, third.T
        col1 = scal[1 + 3 * b + 1]
        col2 = scal[1 + 3 * b + 2]
        for s in range(2):
            cols = pl.ds(s * BLOCK, BLOCK)
            hit1 = jnp.where(col1 == 2 + s, 1.0, 0.0).astype(F32)
            hit2 = jnp.where(col2 == 2 + s, 1.0, 0.0).astype(F32)
            hit3 = jnp.where(col2 == s, 1.0, 0.0).astype(F32)
            rem[0, rows, cols] = (second * hit1).astype(BF)
            rem[1, rows, cols] = (third * hit2).astype(BF)
            rem_t[0, cols, rows] = (second_t * hit1).astype(BF)
            rem_t[1, cols, rows] = (third_t * hit2).astype(BF)
            own[0, rows, cols] = first.astype(BF) if s == b else zero
            own_t[0, cols, rows] = first_t.astype(BF) if s == b else zero
            own[1, rows, cols] = (third * hit3).astype(BF)
            own_t[1, cols, rows] = (third_t * hit3).astype(BF)
    mine = feats[micro].reshape(ROWS, FEAT)
    feats_own[...] = mine
    cot_own[...] = cot[micro].reshape(ROWS, FEAT)
    local = mm(own[0], mine) + mm(own[1], mine)
    base[...] = KEEP * local + RESTART * mine.astype(F32)


def mixed(base, from_left, from_right, rem):
    recv = jnp.concatenate([from_left[...], from_right[...]], axis=0)
    return (base[...] + KEEP * (mm(rem[0], recv) + mm(rem[1], recv))).astype(BF)


def gelu_parts(value):
    return jnp.tanh(C0 * (value + C1 * (value * value * value)))


def gelu_slope(value):
    t = gelu_parts(value)
    return 0.5 * (1.0 + t) + (0.5 * C0) * value * (1.0 - t * t) * (1.0 + (3.0 * C1) * (value * value))


def forward_kernel(k, scal, base, from_left, from_right, rem, weight, out, mix, hidden, to_left, to_right):
    p = mixed(base, from_left, from_right, rem)
    mix[...] = p
    z = (1.0 - beta(k)) * p.astype(F32) + beta(k) * mm(p, weight[...])
    hidden[...] = z
    out[...] = (0.5 * z * (1.0 + gelu_parts(z))).astype(BF).reshape(2, BLOCK, FEAT)
    to_left[...] = out[scal[7]]
    to_right[...] = out[scal[8]]


def forward_rest_kernel(out, feats, own, hidden, base, slope):
    h = out[...].reshape(ROWS, FEAT)
    local = mm(own[0], h) + mm(own[1], h)
    base[...] = KEEP * local + RESTART * feats[...].astype(F32)
    slope[...] = gelu_slope(hidden[...])


def send_back(k, gz, weight, rem_t, gz_round, ga, to_left, to_right):
    gzb = gz.astype(BF)
    gz_round[...] = gzb
    gp = (1.0 - beta(k)) * gz + beta(k) * mm_nt(gzb, weight[...])
    g = (KEEP * gp).astype(BF)
    ga[...] = g
    gb = (mm(rem_t[0], g) + mm(rem_t[1], g)).astype(BF)
    to_left[...] = gb[:BLOCK]
    to_right[...] = gb[BLOCK:]


def top_kernel(k, base, from_left, from_right, rem, weight, cot, rem_t, mix, gz_round, ga, to_left, to_right):
    p = mixed(base, from_left, from_right, rem)
    mix[...] = p
    z = (1.0 - beta(k)) * p.astype(F32) + beta(k) * mm(p, weight[...])
    gz = cot[...].astype(F32) * gelu_slope(z)
    send_back(k, gz, weight, rem_t, gz_round, ga, to_left, to_right)


def gathered(scal, own_grad, from_left, from_right):
    left = from_left[...].astype(F32)
    right = from_right[...].astype(F32)
    parts = []
    for b in range(2):
        hit_left = jnp.where(scal[7] == b, 1.0, 0.0).astype(F32)
        hit_right = jnp.where(scal[8] == b, 1.0, 0.0).astype(F32)
        parts.append(own_grad[b * BLOCK : (b + 1) * BLOCK] + hit_left * left + hit_right * right)
    return jnp.concatenate(parts, axis=0)


def backward_kernel(k, scal, own_grad, from_left, from_right, slope, weight, rem_t, gz_round, ga, to_left, to_right):
    gz = gathered(scal, own_grad, from_left, from_right) * slope[...]
    send_back(k, gz, weight, rem_t, gz_round, ga, to_left, to_right)


def backward_rest_kernel(k, ga, own_t, mix, gz_round, own_grad, weight_grad):
    g = ga[...]
    own_grad[...] = mm(own_t[0], g) + mm(own_t[1], g)
    weight_grad[...] = (beta(k) * mm_tn(mix[...], gz_round[...])).astype(BF)


def last_kernel(k, scal, own_grad, from_left, from_right, slope, mix, weight_grad):
    gz = gathered(scal, own_grad, from_left, from_right) * slope[...]
    weight_grad[...] = (beta(k) * mm_tn(mix[...], gz.astype(BF))).astype(BF)


HALF = spec((BLOCK, FEAT), BF)
ROWS_BF = spec((ROWS, FEAT), BF)
ROWS_F32 = spec((ROWS, FEAT), F32)
GRAD = spec((FEAT, FEAT), BF)
SQUARE = spec((2, ROWS, ROWS), BF)
BACK = (ROWS_BF, ROWS_BF, HALF, HALF)


def exchange(to_left, to_right):
    count = lax.axis_size("x") * lax.axis_size("z")
    up = [(i, (i + 1) % count) for i in range(count)]
    down = [((i + 1) % count, i) for i in range(count)]
    return lax.ppermute(to_right, DOM, up), lax.ppermute(to_left, DOM, down)


def forward(k, scal, base, recv, prep, weight):
    rem, own, feats = prep[0], prep[1], prep[5]
    outs = (spec((2, BLOCK, FEAT), BF), ROWS_BF, ROWS_F32, HALF, HALF)
    out, mix, hidden, left, right = call(
        functools.partial(forward_kernel, k), outs, [scal], [base, *recv, rem, weight], f"forward{k}"
    )
    recv = exchange(left, right)
    base, slope = call(
        forward_rest_kernel, (ROWS_F32, ROWS_F32), [], [out, feats, own, hidden], f"rest{k}"
    )
    return base, recv, mix, slope


def top(k, base, recv, prep, weight):
    rem, rem_t, cot = prep[0], prep[2], prep[6]
    return call(
        functools.partial(top_kernel, k),
        (ROWS_BF,) + BACK,
        [],
        [base, *recv, rem, weight, cot, rem_t],
        f"top{k}",
    )


def back_rest(k, ga, prep, mix, gz_round):
    return call(
        functools.partial(backward_rest_kernel, k),
        (ROWS_F32, GRAD),
        [],
        [ga, prep[3], mix, gz_round],
        f"backrest{k}",
    )


def back(k, scal, own_grad, recv, slope, weight, prep):
    return call(
        functools.partial(backward_kernel, k),
        BACK,
        [scal],
        [own_grad, *recv, slope, weight, prep[2]],
        f"back{k}",
    )


def shards(features, tile_vals, tile_cols, send_lists, section_layers, weights, cotangent):
    micro = lax.axis_index("segment")
    cols = lax.dynamic_index_in_dim(tile_cols[0], micro, 0, keepdims=False)
    sends = lax.dynamic_index_in_dim(send_lists[0, :, :, 0], micro, 0, keepdims=False)
    scal = jnp.concatenate([jnp.full((1,), micro, jnp.int32), cols, sends])
    feats = features.reshape(2, 2, BLOCK, FEAT)
    cots = cotangent.reshape(2, 2, BLOCK, FEAT)
    tiles = tile_vals.reshape(2, 6, BLOCK, BLOCK)

    left, right = call(first_kernel, (HALF, HALF), [scal], [feats], "first")
    recv = exchange(left, right)
    other = lax.ppermute(weights, "segment", [(0, 1), (1, 0)])
    prep = call(
        prep_kernel,
        (SQUARE, SQUARE, SQUARE, SQUARE, ROWS_F32, ROWS_BF, ROWS_BF),
        [scal],
        [tiles, feats, cots],
        "prep",
    )
    base = prep[4]
    low = jnp.where(micro == 0, weights, other)
    high = jnp.where(micro == 0, other, weights)
    two_first = section_layers[0] == 2
    four = (section_layers[0] + section_layers[1]) == 4
    w1, w4 = low[0], high[1]
    w2 = jnp.where(two_first, low[1], high[0])
    w3 = jnp.where(two_first, high[0], high[1])

    base, recv, mix1, slope1 = forward(1, scal, base, recv, prep, w1)
    base, recv, mix2, slope2 = forward(2, scal, base, recv, prep, w2)

    def with_three(scal, base, recv, w3, w4, prep):
        return top(3, base, recv, prep, w3), jnp.zeros((FEAT, FEAT), BF)

    def with_four(scal, base, recv, w3, w4, prep):
        base, recv, mix3, slope3 = forward(3, scal, base, recv, prep, w3)
        mix4, gz, ga, left, right = top(4, base, recv, prep, w4)
        recv = exchange(left, right)
        own_grad, grad4 = back_rest(4, ga, prep, mix4, gz)
        return (mix3, *back(3, scal, own_grad, recv, slope3, w3, prep)), grad4

    (mix3, gz, ga, left, right), grad4 = lax.cond(
        four, with_four, with_three, scal, base, recv, w3, w4, prep
    )
    recv = exchange(left, right)
    own_grad, grad3 = back_rest(3, ga, prep, mix3, gz)
    gz, ga, left, right = back(2, scal, own_grad, recv, slope2, w2, prep)
    recv = exchange(left, right)
    own_grad, grad2 = back_rest(2, ga, prep, mix2, gz)
    grad1 = call(
        functools.partial(last_kernel, 1),
        GRAD,
        [scal],
        [own_grad, *recv, slope1, mix1],
        "last",
    )
    none = jnp.zeros_like(grad1)
    slot1 = jnp.where(two_first, grad2, none)
    slot2 = jnp.where(two_first, grad3, grad2)
    slot3 = jnp.where(two_first, grad4, grad3)
    first = jnp.stack([grad1, slot1])
    second = jnp.stack([slot2, slot3])
    kept = jnp.where(micro == 0, first, second)
    given = jnp.where(micro == 0, second, first)
    taken = lax.ppermute(given, "segment", [(0, 1), (1, 0)])
    part = (kept.astype(F32) + taken.astype(F32)).astype(BF)
    plane = lax.axis_size("x") * lax.axis_size("rep")
    pieces = lax.all_to_all(
        part.reshape(plane, -1, FEAT), PLANE, 0, 0, tiled=True
    )
    piece = jnp.sum(pieces.astype(F32), axis=0).astype(BF)
    depth = lax.axis_size("z")
    step = 1
    while step < depth:
        got = lax.ppermute(piece, "z", [(i, i ^ step) for i in range(depth)])
        piece = (piece.astype(F32) + got.astype(F32)).astype(BF)
        step *= 2
    whole = lax.all_to_all(
        jnp.broadcast_to(piece[None], (plane,) + piece.shape), PLANE, 0, 0, tiled=True
    )
    return whole.reshape(2, FEAT, FEAT).astype(F32)


def solution(mesh):
    sizes = dict(mesh.shape)
    grid = Mesh(
        mesh.devices.reshape(sizes["segment"], 4, sizes["dom"] // 4, sizes["rep"]),
        ("segment", "x", "z", "rep"),
    )
    placed = (
        P("rep", None, DOM, None),
        P("rep", None, DOM, None, None),
        P("rep", None, DOM),
        P("rep", None, DOM, None),
        P(),
        P("segment", None, None),
        P("rep", None, DOM, None),
    )
    return jax.shard_map(
        shards, mesh=grid, in_specs=placed, out_specs=P("segment", None, None), check_vma=False
    )
```

```python
import functools
import math

import jax
import jax.numpy as jnp
import numpy as np
from jax import lax
from jax.experimental import pallas as pl
from jax.experimental.pallas import tpu as pltpu
from jax.sharding import Mesh
from jax.sharding import PartitionSpec as P

BLOCK = 128
ROWS = 256
FEAT = 512
KEEP = 0.9
RESTART = 0.1
STRENGTH = 0.5
C0 = math.sqrt(2.0 / math.pi)
C1 = 0.044715
BF = jnp.bfloat16
F32 = jnp.float32
DOM = ("x", "z")
PLANE = ("x", "rep")


def beta(k):
    return float(np.log(np.float32(STRENGTH / k + 1.0)))


def spec(shape, dtype):
    return jax.ShapeDtypeStruct(shape, dtype)


def call(kernel, outs, scalars, arrays, name, space=pltpu.VMEM, scratch=()):
    smem = [pl.BlockSpec(memory_space=pltpu.SMEM)] * len(scalars)
    held = [pl.BlockSpec(memory_space=space)] * len(arrays)
    if space is pltpu.HBM:
        arrays = [pltpu.with_memory_space_constraint(a, space) for a in arrays]
    return pl.pallas_call(
        kernel,
        out_shape=outs,
        in_specs=smem + held,
        scratch_shapes=list(scratch),
        out_specs=jax.tree.map(lambda _: pl.BlockSpec(memory_space=pltpu.VMEM), outs),
        compiler_params=pltpu.CompilerParams(vmem_limit_bytes=12 * 1024 * 1024),
        name=name,
    )(*scalars, *arrays)


def mm(a, b):
    return jnp.dot(a, b, preferred_element_type=F32)


def mm_nt(a, b):
    return lax.dot_general(a, b, (((1,), (1,)), ((), ())), preferred_element_type=F32)


def mm_tn(a, b):
    return lax.dot_general(a, b, (((0,), (0,)), ((), ())), preferred_element_type=F32)


def first_kernel(micro, sends, feats, to_left, to_right, sems):
    m = micro[0]
    left = pltpu.make_async_copy(feats.at[m, sends[0, m, 0, 0]], to_left, sems.at[0])
    right = pltpu.make_async_copy(feats.at[m, sends[0, m, 1, 0]], to_right, sems.at[1])
    left.start()
    right.start()
    left.wait()
    right.wait()


def prep_kernel(micro, cols, tiles_all, feats, cot, rem, own, rem_t, own_t, base, feats_own, cot_own, tiles, sems):
    m = micro[0]
    get_tiles = pltpu.make_async_copy(tiles_all.at[m], tiles, sems.at[0])
    get_feats = pltpu.make_async_copy(feats.at[m], feats_own, sems.at[1])
    get_cot = pltpu.make_async_copy(cot.at[m], cot_own, sems.at[2])
    get_tiles.start()
    get_feats.start()
    get_cot.start()
    get_tiles.wait()
    zero = jnp.zeros((BLOCK, BLOCK), BF)
    for b in range(2):
        rows = pl.ds(b * BLOCK, BLOCK)
        first = tiles[3 * b].astype(F32)
        second = tiles[3 * b + 1].astype(F32)
        third = tiles[3 * b + 2].astype(F32)
        first_t, second_t, third_t = first.T, second.T, third.T
        col1 = cols[0, m, 3 * b + 1]
        col2 = cols[0, m, 3 * b + 2]
        for s in range(2):
            span = pl.ds(s * BLOCK, BLOCK)
            hit1 = jnp.where(col1 == 2 + s, 1.0, 0.0).astype(F32)
            hit2 = jnp.where(col2 == 2 + s, 1.0, 0.0).astype(F32)
            hit3 = jnp.where(col2 == s, 1.0, 0.0).astype(F32)
            rem[0, rows, span] = (second * hit1).astype(BF)
            rem[1, rows, span] = (third * hit2).astype(BF)
            rem_t[0, span, rows] = (second_t * hit1).astype(BF)
            rem_t[1, span, rows] = (third_t * hit2).astype(BF)
            own[0, rows, span] = first.astype(BF) if s == b else zero
            own_t[0, span, rows] = first_t.astype(BF) if s == b else zero
            own[1, rows, span] = (third * hit3).astype(BF)
            own_t[1, span, rows] = (third_t * hit3).astype(BF)
    get_feats.wait()
    mine = feats_own[...].reshape(ROWS, FEAT)
    local = mm(own[0], mine) + mm(own[1], mine)
    base[...] = KEEP * local + RESTART * mine.astype(F32)
    get_cot.wait()


def mixed(base, from_left, from_right, rem):
    recv = jnp.concatenate([from_left[...], from_right[...]], axis=0)
    return (base[...] + KEEP * (mm(rem[0], recv) + mm(rem[1], recv))).astype(BF)


def gelu_parts(value):
    return jnp.tanh(C0 * (value + C1 * (value * value * value)))


def gelu_slope(value):
    t = gelu_parts(value)
    return 0.5 * (1.0 + t) + (0.5 * C0) * value * (1.0 - t * t) * (1.0 + (3.0 * C1) * (value * value))


def forward_kernel(k, scal, base, from_left, from_right, rem, weight, out, mix, hidden, to_left, to_right):
    p = mixed(base, from_left, from_right, rem)
    mix[...] = p
    z = (1.0 - beta(k)) * p.astype(F32) + beta(k) * mm(p, weight[...])
    hidden[...] = z
    out[...] = (0.5 * z * (1.0 + gelu_parts(z))).astype(BF).reshape(2, BLOCK, FEAT)
    to_left[...] = out[scal[7]]
    to_right[...] = out[scal[8]]


def forward_rest_kernel(out, feats, own, hidden, base, slope):
    h = out[...].reshape(ROWS, FEAT)
    local = mm(own[0], h) + mm(own[1], h)
    base[...] = KEEP * local + RESTART * feats[...].reshape(ROWS, FEAT).astype(F32)
    slope[...] = gelu_slope(hidden[...])


def send_back(k, gz, weight, rem_t, gz_round, ga, to_left, to_right):
    gzb = gz.astype(BF)
    gz_round[...] = gzb
    gp = (1.0 - beta(k)) * gz + beta(k) * mm_nt(gzb, weight[...])
    g = (KEEP * gp).astype(BF)
    ga[...] = g
    gb = (mm(rem_t[0], g) + mm(rem_t[1], g)).astype(BF)
    to_left[...] = gb[:BLOCK]
    to_right[...] = gb[BLOCK:]


def top_kernel(k, base, from_left, from_right, rem, weight, cot, rem_t, mix, gz_round, ga, to_left, to_right):
    p = mixed(base, from_left, from_right, rem)
    mix[...] = p
    z = (1.0 - beta(k)) * p.astype(F32) + beta(k) * mm(p, weight[...])
    gz = cot[...].reshape(ROWS, FEAT).astype(F32) * gelu_slope(z)
    send_back(k, gz, weight, rem_t, gz_round, ga, to_left, to_right)


def gathered(scal, own_grad, from_left, from_right):
    left = from_left[...].astype(F32)
    right = from_right[...].astype(F32)
    parts = []
    for b in range(2):
        hit_left = jnp.where(scal[7] == b, 1.0, 0.0).astype(F32)
        hit_right = jnp.where(scal[8] == b, 1.0, 0.0).astype(F32)
        parts.append(own_grad[b * BLOCK : (b + 1) * BLOCK] + hit_left * left + hit_right * right)
    return jnp.concatenate(parts, axis=0)


def backward_kernel(k, scal, own_grad, from_left, from_right, slope, weight, rem_t, gz_round, ga, to_left, to_right):
    gz = gathered(scal, own_grad, from_left, from_right) * slope[...]
    send_back(k, gz, weight, rem_t, gz_round, ga, to_left, to_right)


def backward_rest_kernel(k, ga, own_t, mix, gz_round, own_grad, weight_grad):
    g = ga[...]
    own_grad[...] = mm(own_t[0], g) + mm(own_t[1], g)
    weight_grad[...] = (beta(k) * mm_tn(mix[...], gz_round[...])).astype(BF)


def last_kernel(k, scal, own_grad, from_left, from_right, slope, mix, weight_grad):
    gz = gathered(scal, own_grad, from_left, from_right) * slope[...]
    weight_grad[...] = (beta(k) * mm_tn(mix[...], gz.astype(BF))).astype(BF)


HALF = spec((BLOCK, FEAT), BF)
ROWS_BF = spec((ROWS, FEAT), BF)
PAIR = spec((2, BLOCK, FEAT), BF)
ROWS_F32 = spec((ROWS, FEAT), F32)
GRAD = spec((FEAT, FEAT), BF)
SQUARE = spec((2, ROWS, ROWS), BF)
BACK = (ROWS_BF, ROWS_BF, HALF, HALF)


def exchange(to_left, to_right):
    count = lax.axis_size("x") * lax.axis_size("z")
    up = [(i, (i + 1) % count) for i in range(count)]
    down = [((i + 1) % count, i) for i in range(count)]
    return lax.ppermute(to_right, DOM, up), lax.ppermute(to_left, DOM, down)


def forward(k, scal, base, recv, prep, weight):
    rem, own, feats = prep[0], prep[1], prep[5]
    outs = (PAIR, ROWS_BF, ROWS_F32, HALF, HALF)
    out, mix, hidden, left, right = call(
        functools.partial(forward_kernel, k), outs, [scal], [base, *recv, rem, weight], f"forward{k}"
    )
    recv = exchange(left, right)
    base, slope = call(
        forward_rest_kernel, (ROWS_F32, ROWS_F32), [], [out, feats, own, hidden], f"rest{k}"
    )
    return base, recv, mix, slope


def top(k, base, recv, prep, weight):
    rem, rem_t, cot = prep[0], prep[2], prep[6]
    return call(
        functools.partial(top_kernel, k),
        (ROWS_BF,) + BACK,
        [],
        [base, *recv, rem, weight, cot, rem_t],
        f"top{k}",
    )


def back_rest(k, ga, prep, mix, gz_round):
    return call(
        functools.partial(backward_rest_kernel, k),
        (ROWS_F32, GRAD),
        [],
        [ga, prep[3], mix, gz_round],
        f"backrest{k}",
    )


def back(k, scal, own_grad, recv, slope, weight, prep):
    return call(
        functools.partial(backward_kernel, k),
        BACK,
        [scal],
        [own_grad, *recv, slope, weight, prep[2]],
        f"back{k}",
    )


def core_sums(micro, slot1, slot2, slot3):
    first = micro == 0
    given = jnp.where(first, slot3, slot1)
    kept = jnp.where(first, slot1, slot3)
    taken = lax.ppermute(given, "segment", [(0, 1), (1, 0)])
    part_b = (kept.astype(F32) + taken.astype(F32)).astype(BF)
    early = lax.ppermute(slot2, "segment", [(0, 1)])

    def share_late(slot0):
        late = lax.ppermute(slot0, "segment", [(1, 0)])
        low = jnp.where(first, slot0, slot2).astype(F32)
        return (low + jnp.where(first, late, early).astype(F32)).astype(BF)

    return part_b, share_late


def along_z(piece):
    depth = lax.axis_size("z")
    half = depth // 2
    value = piece.astype(F32)
    near, far, both = (
        lax.ppermute(piece, "z", [(i, i ^ k) for i in range(depth)]).astype(F32) for k in (1, 2, 3)
    )
    piece = ((value + near) + (far + both)).astype(BF)
    pairs = [(i, half + (i + 2) % half) for i in range(half)]
    got = lax.ppermute(piece, "z", pairs + [(b, a) for a, b in pairs])
    return (piece.astype(F32) + got.astype(F32)).astype(BF)


def shards(features, tile_vals, tile_cols, send_lists, section_layers, weights, cotangent):
    micro = lax.axis_index("segment")
    index = jnp.full((1,), micro, jnp.int32)
    feats = features.reshape(2, 2, BLOCK, FEAT)
    cots = cotangent.reshape(2, 2, BLOCK, FEAT)
    tiles = tile_vals.reshape(2, 6, BLOCK, BLOCK)
    cols = tile_cols[0]
    sends = send_lists[0, :, :, 0]

    left, right = call(
        first_kernel,
        (HALF, HALF),
        [index, send_lists],
        [feats],
        "first",
        pltpu.HBM,
        [pltpu.SemaphoreType.DMA((2,))],
    )
    recv = exchange(left, right)
    other = lax.ppermute(weights, "segment", [(0, 1), (1, 0)])
    prep = call(
        prep_kernel,
        (SQUARE, SQUARE, SQUARE, SQUARE, ROWS_F32, PAIR, PAIR),
        [index, tile_cols],
        [tiles, feats, cots],
        "prep",
        pltpu.HBM,
        [pltpu.VMEM((6, BLOCK, BLOCK), BF), pltpu.SemaphoreType.DMA((3,))],
    )
    base = prep[4]
    w1 = jnp.where(micro == 0, weights[0], other[0])
    late, later_weights, cols, sends, layers, _ = lax.optimization_barrier(
        (index, (weights, other), cols, sends, section_layers, left)
    )
    scal = jnp.concatenate(
        [
            late,
            lax.dynamic_index_in_dim(cols, micro, 0, keepdims=False),
            lax.dynamic_index_in_dim(sends, micro, 0, keepdims=False),
        ]
    )
    two_first = layers[0] == 2
    four = (layers[0] + layers[1]) == 4

    base, recv, mix1, slope1 = forward(1, scal, base, recv, prep, w1)
    (mine, theirs), _ = lax.optimization_barrier((later_weights, slope1))
    low1 = jnp.where(micro == 0, mine[1], theirs[1])
    high0 = jnp.where(micro == 0, theirs[0], mine[0])
    w2 = jnp.where(two_first, low1, high0)
    w4 = jnp.where(micro == 0, theirs[1], mine[1])
    w3 = jnp.where(two_first, high0, w4)
    base, recv, mix2, slope2 = forward(2, scal, base, recv, prep, w2)

    def with_three(scal, base, recv, w3, w4, prep):
        return top(3, base, recv, prep, w3), jnp.zeros((FEAT, FEAT), BF)

    def with_four(scal, base, recv, w3, w4, prep):
        base, recv, mix3, slope3 = forward(3, scal, base, recv, prep, w3)
        mix4, gz, ga, left, right = top(4, base, recv, prep, w4)
        recv = exchange(left, right)
        own_grad, grad4 = back_rest(4, ga, prep, mix4, gz)
        return (mix3, *back(3, scal, own_grad, recv, slope3, w3, prep)), grad4

    (mix3, gz, ga, left, right), grad4 = lax.cond(
        four, with_four, with_three, scal, base, recv, w3, w4, prep
    )
    recv = exchange(left, right)
    own_grad, grad3 = back_rest(3, ga, prep, mix3, gz)
    gz, ga, left, right = back(2, scal, own_grad, recv, slope2, w2, prep)
    recv = exchange(left, right)
    own_grad, grad2 = back_rest(2, ga, prep, mix2, gz)
    none = jnp.zeros_like(grad2)
    slot1 = jnp.where(two_first, grad2, none)
    slot2 = jnp.where(two_first, grad3, grad2)
    slot3 = jnp.where(two_first, grad4, grad3)
    (slot1, slot2, slot3), recv = lax.optimization_barrier(((slot1, slot2, slot3), recv))
    part_b, share_late = core_sums(micro, slot1, slot2, slot3)
    grad1 = call(
        functools.partial(last_kernel, 1),
        GRAD,
        [scal],
        [own_grad, *recv, slope1, mix1],
        "last",
    )
    part = jnp.stack([share_late(grad1), part_b])
    plane = lax.axis_size("x") * lax.axis_size("rep")
    pieces = lax.all_to_all(part.reshape(plane, -1, FEAT), PLANE, 0, 0, tiled=True)
    piece = along_z(jnp.sum(pieces.astype(F32), axis=0).astype(BF))
    whole = lax.all_to_all(
        jnp.broadcast_to(piece[None], (plane,) + piece.shape), PLANE, 0, 0, tiled=True
    )
    return whole.reshape(2, FEAT, FEAT).astype(F32)


def solution(mesh):
    sizes = dict(mesh.shape)
    grid = Mesh(
        mesh.devices.reshape(sizes["segment"], 4, sizes["dom"] // 4, sizes["rep"]),
        ("segment", "x", "z", "rep"),
    )
    placed = (
        P("rep", None, DOM, None),
        P("rep", None, DOM, None, None),
        P("rep", None, DOM),
        P("rep", None, DOM, None),
        P(),
        P("segment", None, None),
        P("rep", None, DOM, None),
    )
    return jax.shard_map(
        shards, mesh=grid, in_specs=placed, out_specs=P("segment", None, None), check_vma=False
    )
```

```python
import functools
import math

import jax
import jax.numpy as jnp
import numpy as np
from jax import lax
from jax.experimental import pallas as pl
from jax.experimental.pallas import tpu as pltpu
from jax.sharding import Mesh
from jax.sharding import PartitionSpec as P

BLOCK = 128
ROWS = 256
FEAT = 512
KEEP = 0.9
RESTART = 0.1
STRENGTH = 0.5
C0 = math.sqrt(2.0 / math.pi)
C1 = 0.044715
BF = jnp.bfloat16
F32 = jnp.float32
DOM = ("x", "z")
PLANE = ("x", "rep")


def beta(k):
    return float(np.log(np.float32(STRENGTH / k + 1.0)))


def spec(shape, dtype):
    return jax.ShapeDtypeStruct(shape, dtype)


def call(kernel, outs, scalars, arrays, name, space=pltpu.VMEM, scratch=(), aliases=None):
    smem = [pl.BlockSpec(memory_space=pltpu.SMEM)] * len(scalars)
    held = [pl.BlockSpec(memory_space=space)] * len(arrays)
    if space is pltpu.HBM:
        arrays = [pltpu.with_memory_space_constraint(a, space) for a in arrays]
    return pl.pallas_call(
        kernel,
        out_shape=outs,
        in_specs=smem + held,
        scratch_shapes=list(scratch),
        input_output_aliases=aliases or {},
        out_specs=jax.tree.map(lambda _: pl.BlockSpec(memory_space=pltpu.VMEM), outs),
        compiler_params=pltpu.CompilerParams(vmem_limit_bytes=12 * 1024 * 1024),
        name=name,
    )(*scalars, *arrays)


def mm(a, b):
    return jnp.dot(a, b, preferred_element_type=F32)


def mm_nt(a, b):
    return lax.dot_general(a, b, (((1,), (1,)), ((), ())), preferred_element_type=F32)


def mm_tn(a, b):
    return lax.dot_general(a, b, (((0,), (0,)), ((), ())), preferred_element_type=F32)


N_FLAGS = 16


def first_kernel(
    micro, sends, cols, tiles_all, feats, cot, to_left, to_right, tiles, feats_own, cot_own, flags, sends_in, cols_in, sems
):
    m = micro[0]
    copies = [
        pltpu.make_async_copy(sends, sends_in, sems.at[0]),
        pltpu.make_async_copy(cols, cols_in, sems.at[1]),
        pltpu.make_async_copy(feats.at[m], feats_own, sems.at[2]),
        pltpu.make_async_copy(tiles_all.at[m], tiles, sems.at[3]),
        pltpu.make_async_copy(cot.at[m], cot_own, sems.at[4]),
    ]
    for copy in copies:
        copy.start()
    copies[0].wait()
    copies[1].wait()

    def put(row, value):
        flags[row : row + 1, :] = jnp.full((1, FEAT), value.astype(F32), F32)

    put(0, sends_in[m, 0])
    put(1, sends_in[m, 1])
    for b in range(2):
        for s in range(2):
            row = 2 * b + s
            put(2 + row, jnp.where(cols_in[m, 3 * b + 1] == 2 + s, 1, 0))
            put(6 + row, jnp.where(cols_in[m, 3 * b + 2] == 2 + s, 1, 0))
            put(10 + row, jnp.where(cols_in[m, 3 * b + 2] == s, 1, 0))
    copies[2].wait()
    to_left[...] = feats_own[sends_in[m, 0]]
    to_right[...] = feats_own[sends_in[m, 1]]
    copies[3].wait()
    copies[4].wait()


def choose(use_own, row, mine, other, out):
    @pl.when(use_own)
    def _():
        out[...] = mine[row]

    @pl.when(jnp.logical_not(use_own))
    def _():
        out[...] = other[row]


def squares(tiles, flags, rem, own):
    zero = jnp.zeros((BLOCK, BLOCK), BF)
    for b in range(2):
        rows = pl.ds(b * BLOCK, BLOCK)
        first, second, third = (tiles[3 * b + i].astype(F32) for i in range(3))
        for s in range(2):
            span = pl.ds(s * BLOCK, BLOCK)
            at = (rows, span)
            hit1, hit2, hit3 = (flags[r : r + 1, :BLOCK] for r in (2 + 2 * b + s, 6 + 2 * b + s, 10 + 2 * b + s))
            rem[(0, *at)] = (second * hit1).astype(BF)
            rem[(1, *at)] = (third * hit2).astype(BF)
            own[(0, *at)] = first.astype(BF) if s == b else zero
            own[(1, *at)] = (third * hit3).astype(BF)


def prep_kernel(micro, tiles, flags, feats, weights, other, rem, own, base, w1):
    squares(tiles, flags, rem, own)
    h = feats[...].reshape(ROWS, FEAT)
    base[...] = KEEP * (mm(own[0], h) + mm(own[1], h)) + RESTART * h.astype(F32)
    choose(micro[0] == 0, 0, weights, other, w1)


def mixed(base, from_left, from_right, rem):
    recv = jnp.concatenate([from_left[...], from_right[...]], axis=0)
    return (base[...] + KEEP * (mm(rem[0], recv) + mm(rem[1], recv))).astype(BF)


def gelu_parts(value):
    return jnp.tanh(C0 * (value + C1 * (value * value * value)))


def gelu_slope(value):
    t = gelu_parts(value)
    return 0.5 * (1.0 + t) + (0.5 * C0) * value * (1.0 - t * t) * (1.0 + (3.0 * C1) * (value * value))


def pick(flags, entry, value):
    return jnp.where(flags[entry : entry + 1, :] > 0.5, value[BLOCK:], value[:BLOCK])


def forward_kernel(k, flags, base, from_left, from_right, rem, weight, out, mix, hidden, to_left, to_right):
    p = mixed(base, from_left, from_right, rem)
    mix[...] = p
    z = (1.0 - beta(k)) * p.astype(F32) + beta(k) * mm(p, weight[...])
    hidden[...] = z
    h = 0.5 * z * (1.0 + gelu_parts(z))
    out[...] = h.astype(BF)
    to_left[...] = pick(flags, 0, h).astype(BF)
    to_right[...] = pick(flags, 1, h).astype(BF)


def rest_kernel(out, feats, own, hidden, base, slope):
    h = out[...]
    local = mm(own[0], h) + mm(own[1], h)
    base[...] = KEEP * local + RESTART * feats[...].reshape(ROWS, FEAT).astype(F32)
    slope[...] = gelu_slope(hidden[...])


def rest1_kernel(
    micro, layers, out, feats, own, hidden, weights, other, base, slope, w2
):
    rest_kernel(out, feats, own, hidden, base, slope)
    two_first = layers[0] == 2
    choose(two_first == (micro[0] == 0), jnp.where(two_first, 1, 0), weights, other, w2)


def rest2_kernel(micro, layers, out, feats, own, hidden, weights, other, base, slope, w3, w4):
    rest_kernel(out, feats, own, hidden, base, slope)
    use_own = micro[0] == 1
    choose(use_own, jnp.where(layers[0] == 2, 0, 1), weights, other, w3)
    choose(use_own, 1, weights, other, w4)


def send_back(k, gz, weight, rem, gz_round, ga, to_left, to_right):
    gzb = gz.astype(BF)
    gz_round[...] = gzb
    gp = (1.0 - beta(k)) * gz + beta(k) * mm_nt(gzb, weight[...])
    g = (KEEP * gp).astype(BF)
    ga[...] = g
    gb = (mm_tn(rem[0], g) + mm_tn(rem[1], g)).astype(BF)
    to_left[...] = gb[:BLOCK]
    to_right[...] = gb[BLOCK:]


def top_kernel(
    k, base, from_left, from_right, rem, weight, cot, mix, gz_round, ga, to_left, to_right, *unwritten
):
    p = mixed(base, from_left, from_right, rem)
    mix[...] = p
    z = (1.0 - beta(k)) * p.astype(F32) + beta(k) * mm(p, weight[...])
    gz = cot[...].reshape(ROWS, FEAT).astype(F32) * gelu_slope(z)
    send_back(k, gz, weight, rem, gz_round, ga, to_left, to_right)


def gathered(flags, own_grad, from_left, from_right):
    left = from_left[...].astype(F32)
    right = from_right[...].astype(F32)
    hit_left, hit_right = flags[0:1, :], flags[1:2, :]
    low = own_grad[:BLOCK] + (1.0 - hit_left) * left + (1.0 - hit_right) * right
    high = own_grad[BLOCK:] + hit_left * left + hit_right * right
    return jnp.concatenate([low, high], axis=0)


def backward_kernel(k, flags, own_grad, from_left, from_right, slope, weight, rem, gz_round, ga, to_left, to_right):
    gz = gathered(flags, own_grad, from_left, from_right) * slope[...]
    send_back(k, gz, weight, rem, gz_round, ga, to_left, to_right)


def backward_rest_kernel(k, ga, own, mix, gz_round, own_grad, weight_grad):
    g = ga[...]
    own_grad[...] = mm_tn(own[0], g) + mm_tn(own[1], g)
    weight_grad[...] = (beta(k) * mm_tn(mix[...], gz_round[...])).astype(BF)


def slots_kernel(micro, layers, ga, own, mix, gz_round, grad3, grad4, own_grad, kept, given):
    g = ga[...]
    own_grad[...] = mm_tn(own[0], g) + mm_tn(own[1], g)
    grad2 = (beta(2) * mm_tn(mix[...], gz_round[...])).astype(BF)
    none = jnp.zeros((FEAT, FEAT), BF)
    two_first = layers[0] == 2
    four = two_first & (layers[1] == 2)

    def fill(low, high):
        @pl.when(two_first)
        def _():
            low[1] = grad2
            high[0] = grad3[...]

        @pl.when(jnp.logical_not(two_first))
        def _():
            low[1] = none
            high[0] = grad2
            high[1] = grad3[...]

        @pl.when(four)
        def _():
            high[1] = grad4[...]

        @pl.when(two_first & jnp.logical_not(four))
        def _():
            high[1] = none

    @pl.when(micro[0] == 0)
    def _():
        fill(kept, given)

    @pl.when(micro[0] == 1)
    def _():
        fill(given, kept)


def last_kernel(micro, flags, own_grad, from_left, from_right, slope, mix, kept_in, given_in, kept, given):
    gz = gathered(flags, own_grad, from_left, from_right) * slope[...]
    grad = (beta(1) * mm_tn(mix[...], gz.astype(BF))).astype(BF)

    @pl.when(micro[0] == 0)
    def _():
        kept[0] = grad

    @pl.when(micro[0] == 1)
    def _():
        given[0] = grad


HALF = spec((BLOCK, FEAT), BF)
ROWS_BF = spec((ROWS, FEAT), BF)
PAIR = spec((2, BLOCK, FEAT), BF)
ROWS_F32 = spec((ROWS, FEAT), F32)
GRAD = spec((FEAT, FEAT), BF)
SLOTS = spec((2, FEAT, FEAT), BF)
SQUARE = spec((2, ROWS, ROWS), BF)
BACK = (ROWS_BF, ROWS_BF, HALF, HALF)


def exchange(to_left, to_right):
    count = lax.axis_size("x") * lax.axis_size("z")
    up = [(i, (i + 1) % count) for i in range(count)]
    down = [((i + 1) % count, i) for i in range(count)]
    return lax.ppermute(to_right, DOM, up), lax.ppermute(to_left, DOM, down)


def forward(k, flags, base, recv, rem, weight):
    outs = (ROWS_BF, ROWS_BF, ROWS_F32, HALF, HALF)
    out, mix, hidden, left, right = call(
        functools.partial(forward_kernel, k), outs, [], [flags, base, *recv, rem, weight], f"forward{k}"
    )
    return out, mix, hidden, exchange(left, right)


def top(k, base, recv, rem, weight, cot, more=()):
    return call(
        functools.partial(top_kernel, k),
        (ROWS_BF, *BACK, *more),
        [],
        [base, *recv, rem, weight, cot],
        f"top{k}",
    )


def back_rest(k, ga, own, mix, gz_round):
    return call(
        functools.partial(backward_rest_kernel, k),
        (ROWS_F32, GRAD),
        [],
        [ga, own, mix, gz_round],
        f"backrest{k}",
    )


def back(k, flags, own_grad, recv, slope, weight, rem):
    return call(
        functools.partial(backward_kernel, k),
        BACK,
        [],
        [flags, own_grad, *recv, slope, weight, rem],
        f"back{k}",
    )


def along_z(piece):
    depth = lax.axis_size("z")
    got = lax.ppermute(piece, "z", [(i, depth - 1 - i) for i in range(depth)])
    piece = (piece.astype(F32) + got.astype(F32)).astype(BF)
    near, far, both = (
        lax.ppermute(piece, "z", [(i, i ^ k) for i in range(depth)]).astype(F32) for k in (1, 2, 3)
    )
    return ((piece.astype(F32) + near) + (far + both)).astype(BF)


def shards(features, tile_vals, tile_cols, send_lists, section_layers, weights, cotangent):
    micro = jnp.full((1,), lax.axis_index("segment"), jnp.int32)
    layers = section_layers
    left, right, tiles, feats, cot, flags = call(
        first_kernel,
        (HALF, HALF, spec((6, BLOCK, BLOCK), BF), PAIR, PAIR, spec((N_FLAGS, FEAT), F32)),
        [micro],
        [
            send_lists.reshape(2, 2),
            tile_cols.reshape(2, 6),
            tile_vals.reshape(2, 6, BLOCK, BLOCK),
            features.reshape(2, 2, BLOCK, FEAT),
            cotangent.reshape(2, 2, BLOCK, FEAT),
        ],
        "first",
        pltpu.HBM,
        [
            pltpu.SMEM((2, 2), jnp.int32),
            pltpu.SMEM((2, 6), jnp.int32),
            pltpu.SemaphoreType.DMA((5,)),
        ],
    )
    recv = exchange(left, right)
    weights, layers, left = lax.optimization_barrier((weights, layers, left))
    four = (layers[0] + layers[1]) == 4
    tiles, _ = lax.optimization_barrier((tiles, four.astype(jnp.int32)))
    other = lax.ppermute(weights, "segment", [(0, 1), (1, 0)])
    rem, own, base, w1 = call(
        prep_kernel,
        (SQUARE, SQUARE, ROWS_F32, GRAD),
        [micro],
        [tiles, flags, feats, weights, other],
        "prep",
    )
    out, mix1, hidden, recv = forward(1, flags, base, recv, rem, w1)
    base, slope1, w2 = call(
        rest1_kernel,
        (ROWS_F32, ROWS_F32, GRAD),
        [micro, layers],
        [out, feats, own, hidden, weights, other],
        "rest1",
    )
    out, mix2, hidden, recv = forward(2, flags, base, recv, rem, w2)
    base, slope2, w3, w4 = call(
        rest2_kernel,
        (ROWS_F32, ROWS_F32, GRAD, GRAD),
        [micro, layers],
        [out, feats, own, hidden, weights, other],
        "rest2",
    )

    def with_three(base, recv, w3, w4):
        *outs, unwritten = top(3, base, recv, rem, w3, cot, (GRAD,))
        return (unwritten, *outs)

    def with_four(base, recv, w3, w4):
        out, mix3, hidden, recv = forward(3, flags, base, recv, rem, w3)
        base, slope3 = call(
            rest_kernel, (ROWS_F32, ROWS_F32), [], [out, feats, own, hidden], "rest3"
        )
        mix4, gz, ga, left, right = top(4, base, recv, rem, w4, cot)
        recv = exchange(left, right)
        own_grad, grad4 = back_rest(4, ga, own, mix4, gz)
        return (grad4, mix3, *back(3, flags, own_grad, recv, slope3, w3, rem))

    grad4, mix3, gz, ga, left, right = lax.cond(four, with_four, with_three, base, recv, w3, w4)
    recv = exchange(left, right)
    own_grad, grad3 = back_rest(3, ga, own, mix3, gz)
    gz, ga, left, right = back(2, flags, own_grad, recv, slope2, w2, rem)
    recv = exchange(left, right)
    own_grad, kept, given = call(
        slots_kernel,
        (ROWS_F32, SLOTS, SLOTS),
        [micro, layers],
        [ga, own, mix2, gz, grad3, grad4],
        "slots",
    )
    kept, given = call(
        last_kernel,
        (SLOTS, SLOTS),
        [micro],
        [flags, own_grad, *recv, slope1, mix1, kept, given],
        "last",
        aliases={7: 0, 8: 1},
    )
    taken = lax.ppermute(given, "segment", [(0, 1), (1, 0)])
    part = (kept.astype(F32) + taken.astype(F32)).astype(BF)
    plane = lax.axis_size("x") * lax.axis_size("rep")
    pieces = lax.all_to_all(part.reshape(plane, -1, FEAT), PLANE, 0, 0, tiled=True)
    piece = along_z(jnp.sum(pieces.astype(F32), axis=0).astype(BF))
    whole = lax.all_to_all(
        jnp.broadcast_to(piece[None], (plane,) + piece.shape), PLANE, 0, 0, tiled=True
    )
    return whole.reshape(2, FEAT, FEAT).astype(F32)


def solution(mesh):
    sizes = dict(mesh.shape)
    grid = Mesh(
        mesh.devices.reshape(sizes["segment"], 4, sizes["dom"] // 4, sizes["rep"]),
        ("segment", "x", "z", "rep"),
    )
    placed = (
        P("rep", None, DOM, None),
        P("rep", None, DOM, None, None),
        P("rep", None, DOM),
        P("rep", None, DOM, None),
        P(),
        P("segment", None, None),
        P("rep", None, DOM, None),
    )
    return jax.shard_map(
        shards, mesh=grid, in_specs=placed, out_specs=P("segment", None, None), check_vma=False
    )
```

```python
import functools
import math

import jax
import jax.numpy as jnp
import numpy as np
from jax import lax
from jax.experimental import pallas as pl
from jax.experimental.pallas import tpu as pltpu
from jax.sharding import Mesh
from jax.sharding import PartitionSpec as P

BLOCK = 128
ROWS = 256
FEAT = 512
KEEP = 0.9
RESTART = 0.1
STRENGTH = 0.5
C0 = math.sqrt(2.0 / math.pi)
C1 = 0.044715
BF = jnp.bfloat16
F32 = jnp.float32
DOM = ("x", "z")
PLANE = ("x", "rep")


def beta(k):
    return float(np.log(np.float32(STRENGTH / k + 1.0)))


def spec(shape, dtype):
    return jax.ShapeDtypeStruct(shape, dtype)


def call(kernel, outs, scalars, arrays, name, space=pltpu.VMEM, scratch=(), aliases=None):
    smem = [pl.BlockSpec(memory_space=pltpu.SMEM)] * len(scalars)
    held = [pl.BlockSpec(memory_space=space)] * len(arrays)
    if space is pltpu.HBM:
        arrays = [pltpu.with_memory_space_constraint(a, space) for a in arrays]
    return pl.pallas_call(
        kernel,
        out_shape=outs,
        in_specs=smem + held,
        scratch_shapes=list(scratch),
        input_output_aliases=aliases or {},
        out_specs=jax.tree.map(lambda _: pl.BlockSpec(memory_space=pltpu.VMEM), outs),
        compiler_params=pltpu.CompilerParams(vmem_limit_bytes=12 * 1024 * 1024),
        name=name,
    )(*scalars, *arrays)


def mm(a, b):
    return jnp.dot(a, b, preferred_element_type=F32)


def mm_nt(a, b):
    return lax.dot_general(a, b, (((1,), (1,)), ((), ())), preferred_element_type=F32)


def mm_tn(a, b):
    return lax.dot_general(a, b, (((0,), (0,)), ((), ())), preferred_element_type=F32)


N_FLAGS = 16


def first_kernel(
    micro, sends, cols, tiles_all, feats, cot, to_left, to_right, tiles, feats_own, cot_own, flags, sends_in, cols_in, sems
):
    m = micro[0]
    copies = [
        pltpu.make_async_copy(sends, sends_in, sems.at[0]),
        pltpu.make_async_copy(cols, cols_in, sems.at[1]),
        pltpu.make_async_copy(feats.at[m], feats_own, sems.at[2]),
        pltpu.make_async_copy(tiles_all.at[m], tiles, sems.at[3]),
        pltpu.make_async_copy(cot.at[m], cot_own, sems.at[4]),
    ]
    for copy in copies:
        copy.start()
    copies[0].wait()
    copies[1].wait()

    def put(row, value):
        flags[row : row + 1, :] = jnp.full((1, FEAT), value.astype(F32), F32)

    put(0, sends_in[m, 0])
    put(1, sends_in[m, 1])
    for b in range(2):
        for s in range(2):
            row = 2 * b + s
            put(2 + row, jnp.where(cols_in[m, 3 * b + 1] == 2 + s, 1, 0))
            put(6 + row, jnp.where(cols_in[m, 3 * b + 2] == 2 + s, 1, 0))
            put(10 + row, jnp.where(cols_in[m, 3 * b + 2] == s, 1, 0))
    copies[2].wait()
    to_left[...] = feats_own[sends_in[m, 0]]
    to_right[...] = feats_own[sends_in[m, 1]]
    copies[3].wait()
    copies[4].wait()


def choose(use_own, row, mine, other, out):
    @pl.when(use_own)
    def _():
        out[...] = mine[row]

    @pl.when(jnp.logical_not(use_own))
    def _():
        out[...] = other[row]


def squares(tiles, flags, rem, own):
    zero = jnp.zeros((BLOCK, BLOCK), BF)
    for b in range(2):
        rows = pl.ds(b * BLOCK, BLOCK)
        first, second, third = (tiles[3 * b + i].astype(F32) for i in range(3))
        for s in range(2):
            span = pl.ds(s * BLOCK, BLOCK)
            at = (rows, span)
            hit1, hit2, hit3 = (flags[r : r + 1, :BLOCK] for r in (2 + 2 * b + s, 6 + 2 * b + s, 10 + 2 * b + s))
            rem[(0, *at)] = (second * hit1).astype(BF)
            rem[(1, *at)] = (third * hit2).astype(BF)
            own[(0, *at)] = first.astype(BF) if s == b else zero
            own[(1, *at)] = (third * hit3).astype(BF)


def prep_kernel(micro, tiles, flags, feats, weights, other, rem, own, base, w1):
    squares(tiles, flags, rem, own)
    h = feats[...].reshape(ROWS, FEAT)
    base[...] = KEEP * (mm(own[0], h) + mm(own[1], h)) + RESTART * h.astype(F32)
    choose(micro[0] == 0, 0, weights, other, w1)


def mixed(base, from_left, from_right, rem):
    recv = jnp.concatenate([from_left[...], from_right[...]], axis=0)
    return (base[...] + KEEP * (mm(rem[0], recv) + mm(rem[1], recv))).astype(BF)


def gelu_parts(value):
    return jnp.tanh(C0 * (value + C1 * (value * value * value)))


def gelu_slope(value):
    t = gelu_parts(value)
    return 0.5 * (1.0 + t) + (0.5 * C0) * value * (1.0 - t * t) * (1.0 + (3.0 * C1) * (value * value))


def pick(flags, entry, value):
    return jnp.where(flags[entry : entry + 1, :] > 0.5, value[BLOCK:], value[:BLOCK])


def forward_kernel(k, flags, base, from_left, from_right, rem, weight, out, mix, hidden, to_left, to_right):
    p = mixed(base, from_left, from_right, rem)
    mix[...] = p
    z = (1.0 - beta(k)) * p.astype(F32) + beta(k) * mm(p, weight[...])
    hidden[...] = z
    h = 0.5 * z * (1.0 + gelu_parts(z))
    out[...] = h.astype(BF)
    to_left[...] = pick(flags, 0, h).astype(BF)
    to_right[...] = pick(flags, 1, h).astype(BF)


def rest_kernel(out, feats, own, hidden, base, slope):
    h = out[...]
    local = mm(own[0], h) + mm(own[1], h)
    base[...] = KEEP * local + RESTART * feats[...].reshape(ROWS, FEAT).astype(F32)
    slope[...] = gelu_slope(hidden[...])


def rest1_kernel(
    micro, layers, out, feats, own, hidden, weights, other, base, slope, w2
):
    rest_kernel(out, feats, own, hidden, base, slope)
    two_first = layers[0] == 2
    choose(two_first == (micro[0] == 0), jnp.where(two_first, 1, 0), weights, other, w2)


def rest2_kernel(micro, layers, out, feats, own, hidden, weights, other, base, slope, w3, w4):
    rest_kernel(out, feats, own, hidden, base, slope)
    use_own = micro[0] == 1
    choose(use_own, jnp.where(layers[0] == 2, 0, 1), weights, other, w3)
    choose(use_own, 1, weights, other, w4)


def send_back(k, gz, weight, rem, gz_round, ga, to_left, to_right):
    gzb = gz.astype(BF)
    gz_round[...] = gzb
    gp = (1.0 - beta(k)) * gz + beta(k) * mm_nt(gzb, weight[...])
    g = (KEEP * gp).astype(BF)
    ga[...] = g
    gb = (mm_tn(rem[0], g) + mm_tn(rem[1], g)).astype(BF)
    to_left[...] = gb[:BLOCK]
    to_right[...] = gb[BLOCK:]


def top_kernel(
    k, base, from_left, from_right, rem, weight, cot, mix, gz_round, ga, to_left, to_right, *unwritten
):
    p = mixed(base, from_left, from_right, rem)
    mix[...] = p
    z = (1.0 - beta(k)) * p.astype(F32) + beta(k) * mm(p, weight[...])
    gz = cot[...].reshape(ROWS, FEAT).astype(F32) * gelu_slope(z)
    send_back(k, gz, weight, rem, gz_round, ga, to_left, to_right)


def gathered(flags, own_grad, from_left, from_right):
    left = from_left[...].astype(F32)
    right = from_right[...].astype(F32)
    hit_left, hit_right = flags[0:1, :], flags[1:2, :]
    low = own_grad[:BLOCK] + (1.0 - hit_left) * left + (1.0 - hit_right) * right
    high = own_grad[BLOCK:] + hit_left * left + hit_right * right
    return jnp.concatenate([low, high], axis=0)


def backward_kernel(k, flags, own_grad, from_left, from_right, slope, weight, rem, gz_round, ga, to_left, to_right):
    gz = gathered(flags, own_grad, from_left, from_right) * slope[...]
    send_back(k, gz, weight, rem, gz_round, ga, to_left, to_right)


def backward_rest_kernel(k, ga, own, mix, gz_round, own_grad, weight_grad):
    g = ga[...]
    own_grad[...] = mm_tn(own[0], g) + mm_tn(own[1], g)
    weight_grad[...] = (beta(k) * mm_tn(mix[...], gz_round[...])).astype(BF)


def slots_kernel(micro, layers, ga, own, mix, gz_round, grad3, grad4, own_grad, kept, given):
    g = ga[...]
    own_grad[...] = mm_tn(own[0], g) + mm_tn(own[1], g)
    grad2 = (beta(2) * mm_tn(mix[...], gz_round[...])).astype(BF)
    none = jnp.zeros((FEAT, FEAT), BF)
    two_first = layers[0] == 2
    four = two_first & (layers[1] == 2)

    def fill(low, high):
        @pl.when(two_first)
        def _():
            low[1] = grad2
            high[0] = grad3[...]

        @pl.when(jnp.logical_not(two_first))
        def _():
            low[1] = none
            high[0] = grad2
            high[1] = grad3[...]

        @pl.when(four)
        def _():
            high[1] = grad4[...]

        @pl.when(two_first & jnp.logical_not(four))
        def _():
            high[1] = none

    @pl.when(micro[0] == 0)
    def _():
        fill(kept, given)

    @pl.when(micro[0] == 1)
    def _():
        fill(given, kept)


def last_kernel(micro, flags, own_grad, from_left, from_right, slope, mix, kept_in, given_in, kept, given):
    gz = gathered(flags, own_grad, from_left, from_right) * slope[...]
    grad = (beta(1) * mm_tn(mix[...], gz.astype(BF))).astype(BF)

    @pl.when(micro[0] == 0)
    def _():
        kept[0] = grad

    @pl.when(micro[0] == 1)
    def _():
        given[0] = grad


PIECES = 8


def widen_kernel(source, out, wide, sems):
    rows = source.shape[0] // PIECES
    copies = []
    for i in range(PIECES):
        span = pl.ds(i * rows, rows)
        wide[span, :] = source[span, :].astype(F32)
        copies.append(pltpu.make_async_copy(wide.at[span, :], out.at[span, :], sems.at[i]))
        copies[-1].start()
    for copy in copies:
        copy.wait()


HALF = spec((BLOCK, FEAT), BF)
ROWS_BF = spec((ROWS, FEAT), BF)
PAIR = spec((2, BLOCK, FEAT), BF)
ROWS_F32 = spec((ROWS, FEAT), F32)
GRAD = spec((FEAT, FEAT), BF)
SLOTS = spec((2, FEAT, FEAT), BF)
SQUARE = spec((2, ROWS, ROWS), BF)
BACK = (ROWS_BF, ROWS_BF, HALF, HALF)


def exchange(to_left, to_right):
    count = lax.axis_size("x") * lax.axis_size("z")
    up = [(i, (i + 1) % count) for i in range(count)]
    down = [((i + 1) % count, i) for i in range(count)]
    return lax.ppermute(to_right, DOM, up), lax.ppermute(to_left, DOM, down)


def forward(k, flags, base, recv, rem, weight):
    outs = (ROWS_BF, ROWS_BF, ROWS_F32, HALF, HALF)
    out, mix, hidden, left, right = call(
        functools.partial(forward_kernel, k), outs, [], [flags, base, *recv, rem, weight], f"forward{k}"
    )
    return out, mix, hidden, exchange(left, right)


def top(k, base, recv, rem, weight, cot, more=()):
    return call(
        functools.partial(top_kernel, k),
        (ROWS_BF, *BACK, *more),
        [],
        [base, *recv, rem, weight, cot],
        f"top{k}",
    )


def back_rest(k, ga, own, mix, gz_round):
    return call(
        functools.partial(backward_rest_kernel, k),
        (ROWS_F32, GRAD),
        [],
        [ga, own, mix, gz_round],
        f"backrest{k}",
    )


def back(k, flags, own_grad, recv, slope, weight, rem):
    return call(
        functools.partial(backward_kernel, k),
        BACK,
        [],
        [flags, own_grad, *recv, slope, weight, rem],
        f"back{k}",
    )


def along_z(piece):
    depth = lax.axis_size("z")
    got = lax.ppermute(piece, "z", [(i, depth - 1 - i) for i in range(depth)])
    piece = (piece.astype(F32) + got.astype(F32)).astype(BF)
    near, far, both = (
        lax.ppermute(piece, "z", [(i, i ^ k) for i in range(depth)]).astype(F32) for k in (1, 2, 3)
    )
    return ((piece.astype(F32) + near) + (far + both)).astype(BF)


def shards(features, tile_vals, tile_cols, send_lists, section_layers, weights, cotangent):
    micro = jnp.full((1,), lax.axis_index("segment"), jnp.int32)
    layers = section_layers
    left, right, tiles, feats, cot, flags = call(
        first_kernel,
        (HALF, HALF, spec((6, BLOCK, BLOCK), BF), PAIR, PAIR, spec((N_FLAGS, FEAT), F32)),
        [micro],
        [
            send_lists.reshape(2, 2),
            tile_cols.reshape(2, 6),
            tile_vals.reshape(2, 6, BLOCK, BLOCK),
            features.reshape(2, 2, BLOCK, FEAT),
            cotangent.reshape(2, 2, BLOCK, FEAT),
        ],
        "first",
        pltpu.HBM,
        [
            pltpu.SMEM((2, 2), jnp.int32),
            pltpu.SMEM((2, 6), jnp.int32),
            pltpu.SemaphoreType.DMA((5,)),
        ],
    )
    recv = exchange(left, right)
    weights, layers, left = lax.optimization_barrier((weights, layers, left))
    four = (layers[0] + layers[1]) == 4
    tiles, _ = lax.optimization_barrier((tiles, four.astype(jnp.int32)))
    other = lax.ppermute(weights, "segment", [(0, 1), (1, 0)])
    rem, own, base, w1 = call(
        prep_kernel,
        (SQUARE, SQUARE, ROWS_F32, GRAD),
        [micro],
        [tiles, flags, feats, weights, other],
        "prep",
    )
    out, mix1, hidden, recv = forward(1, flags, base, recv, rem, w1)
    base, slope1, w2 = call(
        rest1_kernel,
        (ROWS_F32, ROWS_F32, GRAD),
        [micro, layers],
        [out, feats, own, hidden, weights, other],
        "rest1",
    )
    out, mix2, hidden, recv = forward(2, flags, base, recv, rem, w2)
    base, slope2, w3, w4 = call(
        rest2_kernel,
        (ROWS_F32, ROWS_F32, GRAD, GRAD),
        [micro, layers],
        [out, feats, own, hidden, weights, other],
        "rest2",
    )

    def with_three(base, recv, w3, w4):
        *outs, unwritten = top(3, base, recv, rem, w3, cot, (GRAD,))
        return (unwritten, *outs)

    def with_four(base, recv, w3, w4):
        out, mix3, hidden, recv = forward(3, flags, base, recv, rem, w3)
        base, slope3 = call(
            rest_kernel, (ROWS_F32, ROWS_F32), [], [out, feats, own, hidden], "rest3"
        )
        mix4, gz, ga, left, right = top(4, base, recv, rem, w4, cot)
        recv = exchange(left, right)
        own_grad, grad4 = back_rest(4, ga, own, mix4, gz)
        return (grad4, mix3, *back(3, flags, own_grad, recv, slope3, w3, rem))

    grad4, mix3, gz, ga, left, right = lax.cond(four, with_four, with_three, base, recv, w3, w4)
    recv = exchange(left, right)
    own_grad, grad3 = back_rest(3, ga, own, mix3, gz)
    gz, ga, left, right = back(2, flags, own_grad, recv, slope2, w2, rem)
    recv = exchange(left, right)
    own_grad, kept, given = call(
        slots_kernel,
        (ROWS_F32, SLOTS, SLOTS),
        [micro, layers],
        [ga, own, mix2, gz, grad3, grad4],
        "slots",
    )
    kept, given = call(
        last_kernel,
        (SLOTS, SLOTS),
        [micro],
        [flags, own_grad, *recv, slope1, mix1, kept, given],
        "last",
        aliases={7: 0, 8: 1},
    )
    taken = lax.ppermute(given, "segment", [(0, 1), (1, 0)])
    part = (kept.astype(F32) + taken.astype(F32)).astype(BF)
    plane = lax.axis_size("x") * lax.axis_size("rep")
    pieces = lax.all_to_all(part.reshape(plane, -1, FEAT), PLANE, 0, 0, tiled=True)
    piece = along_z(jnp.sum(pieces.astype(F32), axis=0).astype(BF))
    whole = lax.all_to_all(
        jnp.broadcast_to(piece[None], (plane,) + piece.shape), PLANE, 0, 0, tiled=True
    )
    flat = whole.reshape(2 * FEAT, FEAT)
    wide = pl.pallas_call(
        widen_kernel,
        out_shape=spec(flat.shape, F32),
        in_specs=[pl.BlockSpec(memory_space=pltpu.VMEM)],
        out_specs=pl.BlockSpec(memory_space=pltpu.HBM),
        scratch_shapes=[pltpu.VMEM(flat.shape, F32), pltpu.SemaphoreType.DMA((PIECES,))],
        compiler_params=pltpu.CompilerParams(vmem_limit_bytes=12 * 1024 * 1024),
        name="widen",
    )(flat)
    return wide.reshape(2, FEAT, FEAT)


def solution(mesh):
    sizes = dict(mesh.shape)
    grid = Mesh(
        mesh.devices.reshape(sizes["segment"], 4, sizes["dom"] // 4, sizes["rep"]),
        ("segment", "x", "z", "rep"),
    )
    placed = (
        P("rep", None, DOM, None),
        P("rep", None, DOM, None, None),
        P("rep", None, DOM),
        P("rep", None, DOM, None),
        P(),
        P("segment", None, None),
        P("rep", None, DOM, None),
    )
    return jax.shard_map(
        shards, mesh=grid, in_specs=placed, out_specs=P("segment", None, None), check_vma=False
    )
```
